128 devices in a mesh: client: 4 (over y_hi, core), mp: 32 (over x, z, y_lo).
Axes of the slice: x: 4, y: 4 (y_hi: 2, y_lo: 2; y = y_hi * 2 + y_lo), z: 4, core: 2. Of those that a mesh axis runs over, the one named last changes fastest.
Arguments:
- tokens: bfloat16 [5120, 4096], P(('client', 'mp')), may hold values from -6 to 6
- out_grad: bfloat16 [5120, 4096], P(('client', 'mp'))
- gate_weight: bfloat16 [4096, 14336], P(None, 'mp')
- up_weight: bfloat16 [4096, 14336], P('client', 'mp'), may hold values from -0.09375 to 0.09375
- down_weight: bfloat16 [4096, 14336], P('client', 'mp'), may hold values from -0.046875 to 0.046875
- counts: int32 [4], replicated, may hold values from 1 to 999
- noise: bfloat16 [2, 4096, 14336], P(None, 'client', 'mp'), may hold values from -3 to 3
- first_moment: float32 [2, 4096, 14336], P(None, 'client', 'mp'), may hold values from -2 to 2
- second_moment: float32 [2, 4096, 14336], P(None, 'client', 'mp'), may hold values from 0.01 to 1
Outputs:
- new_first: float32 [2, 4096, 14336], P(None, 'client', 'mp')
- new_second: float32 [2, 4096, 14336], P(None, 'client', 'mp')
- server_step: float32 [2, 4096, 14336], P(None, 'client', 'mp')
The draws below stay inside these ranges and needn't reach their ends.
All inputs are finite; a program needn't handle non-finite values.
Results may differ from the reference program's by a relative error of at most 0.0019.
Values may be sent and summed in bfloat16 or wider, within the bound.
No kernel may reach another device: no remote copies, remote signals or barrier semaphores. Data moves between devices by JAX's collectives and lax.ppermute only.
A program may use at most 512 MiB of HBM per device.

```python
import math
import jax
import jax.numpy as jnp

D = 4096
FF = 14336
TOK = 1280
CLIENTS = 4
TOKENS = 5120


def draw_out_grad(key, part):
    key = jax.random.fold_in(key, 23)
    first_key, second_key = jax.random.split(key, 2)
    member = jnp.arange(CLIENTS * TOK, dtype=jnp.int32) // TOK
    position = member.astype(jnp.float32) / max(CLIENTS - 1, 1)
    jitter = jax.random.uniform(second_key, (CLIENTS,), jnp.float32, 0.8, 1.25)[member]
    level = 10.0 ** (-1.0 + 2.0 * position)
    values = jax.random.truncated_normal(first_key, -4.0, 4.0, (CLIENTS * TOK, D), jnp.float32)
    return (values * (level * jitter)[:, None]).astype(jnp.bfloat16)


def draw_gate_weight(key, part):
    key = jax.random.fold_in(key, 11)
    values = jax.random.truncated_normal(key, -3.0, 3.0, (D, FF), jnp.float32)
    column = jnp.arange(FF, dtype=jnp.float32) / max(FF - 1, 1)
    growth = 1.0 + 2.0 * column
    return (values * growth[None, :] * D ** (-0.5)).astype(jnp.bfloat16)


def set_ends(array, own_key, least, largest):
    index_at = [jax.random.randint(jax.random.fold_in(own_key, axis), (), 0, length) for axis, length in enumerate(array.shape)]
    main_axis = array.shape.index(max(array.shape))
    next_to = index_at[:main_axis] + [(index_at[main_axis] + 1) % array.shape[main_axis]] + index_at[main_axis + 1:]
    return array.at[tuple(index_at)].set(least).at[tuple(next_to)].set(largest)


def block_scale(stream_key, dims, cuts, least, top_value):
    gain = 1.0
    for dim, shards_of in cuts:
        heights = jax.random.uniform(jax.random.fold_in(jax.random.fold_in(stream_key, 6), dim), (shards_of,), jnp.float32, least / len(cuts), top_value / len(cuts))
        gain = gain * jnp.repeat(jnp.exp(heights), dims[dim] // shards_of).reshape((-1,) + (1,) * (len(dims) - 1 - dim))
    return gain


def centred(own_key, shape, spread, most, cuts=(), kind=jnp.bfloat16):
    gain = block_scale(own_key, shape, cuts, -0.22, 0.18) if cuts else 1.0
    values = jax.random.normal(own_key, shape, jnp.float32) * spread * gain
    return jnp.minimum(jnp.maximum(values, -most), most).astype(kind)


def setup_inputs(seed: int = 0) -> dict:
    streams_of = jax.random.split(jax.random.key(seed), 10)
    tokens = centred(streams_of[0], (TOKENS, D), 1.0, 6.0, ((0, 128),))
    out_grad = draw_out_grad(jax.random.fold_in(streams_of[9], 71), 0)
    gate_weight = draw_gate_weight(jax.random.fold_in(streams_of[9], 71), 0)
    up_weight = centred(streams_of[3], (D, FF), D ** -0.5, 0.09375, ((0, 4), (1, 32)))
    down_weight = centred(streams_of[4], (D, FF), FF ** -0.5, 0.046875, ((0, 4), (1, 32)))
    counts = set_ends(jax.random.randint(streams_of[5], (CLIENTS,), 1, 1000), jax.random.fold_in(streams_of[5], 1), 1, 999).astype(jnp.int32)
    noise = centred(streams_of[6], (2, D, FF), 0.5, 3.0, ((1, 4), (2, 32)))
    first_moment = centred(streams_of[7], (2, D, FF), 0.3, 2.0, ((1, 4), (2, 32)), jnp.float32)
    second_moment = jnp.clip(jnp.exp(math.log(1.0) - 4.6051702 * jax.random.uniform(streams_of[8], (2, D, FF), jnp.float32) ** block_scale(streams_of[8], (2, D, FF), ((1, 4), (2, 32)), -0.2, 0.2)), 0.01, 1.0)
    return dict(tokens=tokens, out_grad=out_grad, gate_weight=gate_weight, up_weight=up_weight, down_weight=down_weight, counts=counts, noise=noise, first_moment=first_moment, second_moment=second_moment)


def reference(tokens, out_grad, gate_weight, up_weight, down_weight, counts, noise, first_moment, second_moment):
    weights = counts.astype(jnp.float32)
    shares = weights / jnp.sum(weights)
    clip_bound = math.sqrt(2.0 * D * FF * TOK)
    average = noise.astype(jnp.float32)
    for member in range(CLIENTS):
        client_rows = tokens[member * TOK:(member + 1) * TOK]
        client_grads = out_grad[member * TOK:(member + 1) * TOK]
        gate_act = jnp.dot(client_rows, gate_weight, preferred_element_type=jnp.float32)
        up_act = jnp.dot(client_rows, up_weight, preferred_element_type=jnp.float32)
        back_grad = jnp.dot(client_grads, down_weight, preferred_element_type=jnp.float32)
        gate_silu = jax.nn.silu(gate_act)
        hidden = (gate_silu * up_act).astype(jnp.bfloat16)
        up_input = (back_grad * gate_silu).astype(jnp.bfloat16)
        up_delta = jnp.dot(client_rows.T, up_input, preferred_element_type=jnp.float32)
        down_delta = jnp.dot(client_grads.T, hidden, preferred_element_type=jnp.float32)
        squared = jnp.sum(up_delta * up_delta) + jnp.sum(down_delta * down_delta)
        weighting = shares[member] * (clip_bound / jnp.maximum(jnp.sqrt(squared), clip_bound))
        average = average + weighting * jnp.stack([up_delta, down_delta])
    new_first = 0.9 * first_moment + 0.1 * average
    new_second = 0.99 * second_moment + 0.01 * average * average
    server_step = new_first / (jnp.sqrt(new_second) + 0.001)
    return (new_first, new_second, server_step)
```

```python
import math

import jax
import jax.numpy as jnp
from jax import lax
from jax.sharding import PartitionSpec as P

NX, NZ, NY = 4, 4, 2


def place(x, z, y):
    return (x % NX) * (NZ * NY) + (z % NZ) * NY + y % NY


def moves(dx=0, dz=0, dy=0):
    return [
        (place(x, z, y), place(x + dx, z + dz, y + dy))
        for x in range(NX)
        for z in range(NZ)
        for y in range(NY)
    ]


def send(value, **by):
    return lax.ppermute(value, "mp", moves(**by))


def swap_core(value):
    return lax.ppermute(value, "client", [(c, c ^ 1) for c in range(4)])


def swap_far(value):
    return lax.ppermute(value, "client", [(c, c ^ 2) for c in range(4)])


def ring(block, axis):
    half = block.shape[0] // 2
    below = send(block, **{axis: 1})
    above = send(block, **{axis: -1})
    far_low = send(below[:half], **{axis: 1})
    far_high = send(above[half:], **{axis: -1})
    return block, below, above, jnp.concatenate([far_low, far_high], axis=0)


def rows_dot(rows, weight):
    return lax.dot_general(rows, weight, (((1,), (0,)), ((), ())), preferred_element_type=jnp.float32)


def inner_t(units, rows):
    return lax.dot_general(units, rows, (((0,), (0,)), ((), ())), preferred_element_type=jnp.float32)


def total_over_mp(value):
    for by in (dict(dy=1), dict(dx=1), dict(dx=2), dict(dz=1), dict(dz=2)):
        if by == dict(dx=1) or by == dict(dz=1):
            axis = "dx" if "dx" in by else "dz"
            value = value + lax.ppermute(value, "mp", flips(axis, 1))
        elif by == dict(dx=2) or by == dict(dz=2):
            axis = "dx" if "dx" in by else "dz"
            value = value + lax.ppermute(value, "mp", flips(axis, 2))
        else:
            value = value + send(value, **by)
    return value


def flips(axis, bit):
    out = []
    for x in range(NX):
        for z in range(NZ):
            for y in range(NY):
                to = place(x ^ bit, z, y) if axis == "dx" else place(x, z ^ bit, y)
                out.append((place(x, z, y), to))
    return out


def local(tokens, out_grad, gate_weight, up_weight, down_weight, counts, noise, first_moment, second_moment):
    model_width = tokens.shape[1]
    local_units = gate_weight.shape[1]
    hidden_units = local_units * lax.axis_size("mp")
    token_count = tokens.shape[0] * lax.axis_size("mp")
    member = lax.axis_index("client")
    core, far = member % 2, member // 2
    width = model_width // 4

    up_all = lax.all_gather(up_weight, "client", axis=0, tiled=True)
    down_all = lax.all_gather(down_weight, "client", axis=0, tiled=True)

    x2 = jnp.concatenate([tokens, send(tokens, dy=1)], axis=0)
    y2 = jnp.concatenate([out_grad, send(out_grad, dy=1)], axis=0)
    x_line = jnp.concatenate(ring(x2, "dx"), axis=0)
    y_line = jnp.concatenate(ring(y2, "dz"), axis=0)
    x_groups = ring(x_line, "dz")
    y_groups = ring(y_line, "dx")
    gate = jnp.stack([rows_dot(g, gate_weight) for g in x_groups])
    up = jnp.stack([rows_dot(g, up_all) for g in x_groups])
    back = jnp.stack([rows_dot(g, down_all) for g in y_groups])
    n = local_units
    silu = jax.nn.silu(gate)
    hidden = (silu * up).astype(jnp.bfloat16)
    back = back.reshape(4, 4, -1, n).swapaxes(0, 1).reshape(4, -1, n)
    up_input = (back * silu).astype(jnp.bfloat16)
    hidden = hidden.reshape(4, 4, -1, n).swapaxes(0, 1).reshape(-1, n)
    up_input = up_input.reshape(-1, n)
    x_all = jnp.concatenate(x_groups, axis=0)
    y_all = jnp.concatenate(y_groups, axis=0)
    up_delta = inner_t(up_input, x_all)
    down_delta = inner_t(hidden, y_all)
    squared = jnp.sum(up_delta * up_delta) + jnp.sum(down_delta * down_delta)

    def part(delta, k):
        return lax.dynamic_index_in_dim(delta.reshape(n, 2, 2, width), k, 2, keepdims=False)

    deltas = (up_delta, down_delta)
    received = [swap_core(part(d, 1 - core)) for d in deltas]
    own = [part(d, core) for d in deltas]
    clip_bound = math.sqrt(2.0 * model_width * hidden_units * token_count)
    weights = counts.astype(jnp.float32)
    shares = weights / jnp.sum(weights)
    client_total = total_over_mp(jnp.full((8, 128), squared, jnp.float32))
    other_total = swap_core(client_total)
    norm_own, norm_other = jnp.sqrt(client_total[0, 0]), jnp.sqrt(other_total[0, 0])
    w_own = shares[member] * (clip_bound / jnp.maximum(norm_own, clip_bound))
    w_other = shares[member ^ 1] * (clip_bound / jnp.maximum(norm_other, clip_bound))
    most = w_own * norm_own + w_other * norm_other
    scale = jnp.where(most > 0.0, jnp.exp2(14.0 - jnp.ceil(jnp.log2(jnp.where(most > 0.0, most, 1.0)))), 1.0)
    their_scale = swap_far(jnp.full((8, 128), scale, jnp.float32))[0, 0]
    results = []
    for i in range(2):
        total = w_own * own[i] + w_other * received[i]
        away = lax.dynamic_index_in_dim(total, 1 - far, 1, keepdims=False)
        here = lax.dynamic_index_in_dim(total, far, 1, keepdims=False)
        arrived = swap_far((away * scale).astype(jnp.float16)).astype(jnp.float32) / their_scale
        average = noise[i].T.astype(jnp.float32) + (here + arrived)
        new_first = 0.9 * first_moment[i].T + 0.1 * average
        new_second = 0.99 * second_moment[i].T + 0.01 * average * average
        results.append((new_first, new_second, new_first / (jnp.sqrt(new_second) + 0.001)))
    return tuple(jnp.stack([results[0][j].T, results[1][j].T]) for j in range(3))


def solution(mesh):
    state = P(None, "client", "mp")
    placed = (
        P(("client", "mp"), None),
        P(("client", "mp"), None),
        P(None, "mp"),
        P("client", "mp"),
        P("client", "mp"),
        P(),
        state,
        state,
        state,
    )
    return jax.shard_map(local, mesh=mesh, in_specs=placed, out_specs=(state,) * 3, check_vma=False)
```

```python
import math

import jax
import jax.numpy as jnp
from jax import lax
from jax.experimental import pallas as pl
from jax.experimental.pallas import tpu as pltpu
from jax.sharding import PartitionSpec as P

NX, NZ, NY = 4, 4, 2
BF16, F32 = jnp.bfloat16, jnp.float32
CORNER = (slice(0, 8), slice(0, 128))


def place(x, z, y):
    return (x % NX) * (NZ * NY) + (z % NZ) * NY + y % NY


def pairs(to):
    return [(place(x, z, y), place(*to(x, z, y))) for x in range(NX) for z in range(NZ) for y in range(NY)]


def send(value, dx=0, dz=0, dy=0):
    return lax.ppermute(value, "mp", pairs(lambda x, z, y: (x + dx, z + dz, y + dy)))


def flip(value, bx=0, bz=0, by=0):
    return lax.ppermute(value, "mp", pairs(lambda x, z, y: (x ^ bx, z ^ bz, y ^ by)))


def swap_core(value):
    return lax.ppermute(value, "client", [(c, c ^ 1) for c in range(4)])


def swap_far(value):
    return lax.ppermute(value, "client", [(c, c ^ 2) for c in range(4)])


def token(*others):
    corners = sum(jnp.abs(other[:8, :128].astype(F32)) for other in others)
    return swap_core(swap_core(jnp.minimum(corners, 0.0)))


def held(value, zeros):
    return value.at[:16, :128].add(jnp.concatenate([zeros, zeros]).astype(value.dtype))


def last_zeros(line):
    quarter = line.shape[0] // 4
    ends = [jnp.abs(line[at : at + 8, :128].astype(F32)) for at in (3 * quarter, 4 * quarter - 16)]
    return jnp.minimum(ends[0] + ends[1], 0.0)


def ring(block, axis):
    half = block.shape[0] // 2
    below = send(block, **{axis: 1})
    above = send(block, **{axis: -1})
    return [block, below, above, below[:half], above[half:]]


def far_block(low, high, axis):
    return jnp.concatenate([send(low, **{axis: 1}), send(high, **{axis: -1})], axis=0)


def line_of(own, axis):
    *blocks, low, high = ring(jnp.concatenate([own, send(own, dy=1)], axis=0), axis)
    return jnp.concatenate([*blocks, far_block(low, high, axis)], axis=0)


def rows_dot(rows, weight):
    return lax.dot_general(rows, weight, (((1,), (0,)), ((), ())), preferred_element_type=F32)


def activations(gates, ups, backs, cut):
    flat = [a for group in zip(gates, ups, backs) for a in group]
    units = flat[0].shape[1]
    rows = sum(a.shape[0] for a in gates)

    def kernel(*refs):
        ins, (up_input, hidden) = refs[: len(flat)], refs[len(flat) :]
        for i in range(4):
            for j in range(4):
                here, there = slice(j * cut, (j + 1) * cut), slice(i * cut, (i + 1) * cut)
                gate = ins[3 * i][here, :]
                silu = gate / (1.0 + jnp.exp(-gate))
                up_input[(4 * i + j) * cut : (4 * i + j + 1) * cut, :] = (ins[3 * j + 2][there, :] * silu).astype(BF16)
                hidden[(4 * j + i) * cut : (4 * j + i + 1) * cut, :] = (silu * ins[3 * i + 1][here, :]).astype(BF16)

    whole = pl.BlockSpec(memory_space=pltpu.VMEM)
    return pl.pallas_call(
        kernel,
        in_specs=[whole] * len(flat),
        out_specs=[whole] * 2,
        out_shape=[jax.ShapeDtypeStruct((rows, units), BF16)] * 2,
        compiler_params=pltpu.CompilerParams(vmem_limit_bytes=24 * 2**20),
        cost_estimate=pl.CostEstimate(flops=10 * rows * units, bytes_accessed=16 * rows * units, transcendentals=rows * units),
    )(*flat)


def deltas(xs, ys, up_input, hidden, columns, width, block=512):
    count, units, rows = len(xs), up_input.shape[1], up_input.shape[0]

    def kernel(_, *refs):
        x, y = refs[:count], refs[count : 2 * count]
        up_ref, hidden_ref, up_out, down_out, squares = refs[2 * count :]

        @pl.when((pl.program_id(0) == 0) & (pl.program_id(1) == 0))
        def _():
            squares[...] = jnp.zeros_like(squares)

        for left, pieces, out in ((up_ref, x, up_out), (hidden_ref, y, down_out)):
            right = jnp.concatenate([piece[...] for piece in pieces], axis=0)
            value = lax.dot_general(left[...], right, (((0,), (0,)), ((), ())), preferred_element_type=F32)
            out[0] = value
            folded = (value * value).reshape(units // 8, 8, block).sum(axis=0)
            squares[...] += sum(folded[:, 128 * i : 128 * (i + 1)] for i in range(block // 128))

    per = width // block
    read = lambda i, j, at: (0, at[i] * per + j)
    fixed = lambda i, j, at: (0, 0)
    return pl.pallas_call(
        kernel,
        grid_spec=pltpu.PrefetchScalarGridSpec(
            num_scalar_prefetch=1,
            grid=(2, per),
            in_specs=[pl.BlockSpec((p.shape[0], block), read) for p in (*xs, *ys)]
            + [pl.BlockSpec((rows, units), fixed)] * 2,
            out_specs=[pl.BlockSpec((1, units, block), lambda i, j, at: (i, 0, j))] * 2
            + [pl.BlockSpec((8, 128), fixed)],
        ),
        out_shape=[jax.ShapeDtypeStruct((2, units, width), F32)] * 2 + [jax.ShapeDtypeStruct((8, 128), F32)],
        compiler_params=pltpu.CompilerParams(vmem_limit_bytes=40 * 2**20),
        cost_estimate=pl.CostEstimate(
            flops=8 * rows * units * width, bytes_accessed=8 * rows * width + 16 * units * width, transcendentals=0
        ),
    )(columns, *xs, *ys, up_input, hidden)


def adam(index, row, factors, keep, received, arrived, noise, first, second, outs, block=64):
    units, width = arrived.shape
    base = row // block

    def kernel(factors, keep, received, arrived, noise, first, second, *refs):
        new_first, new_second, step = refs[-3:]
        average = noise[0].astype(F32) + (
            (factors[0] * keep[0] + factors[1] * received[0]) + arrived[...] * factors[2]
        )
        moment = 0.9 * first[0] + 0.1 * average
        spread = 0.99 * second[0] + 0.01 * average * average
        new_first[0] = moment
        new_second[0] = spread
        step[0] = moment / (jnp.sqrt(spread) + 0.001)

    zero = pl.BlockSpec((1, block, width), lambda i: (0, base + i, 0))
    mine = pl.BlockSpec((1, block, width), lambda i: (index, base + i, 0))
    given = () if outs is None else tuple(outs)
    return pl.pallas_call(
        kernel,
        grid=(units // block,),
        in_specs=[
            pl.BlockSpec(memory_space=pltpu.SMEM),
            zero,
            zero,
            pl.BlockSpec((block, width), lambda i: (i, 0)),
            mine,
            mine,
            mine,
        ]
        + [pl.BlockSpec(memory_space=pl.ANY)] * len(given),
        out_specs=[mine] * 3,
        out_shape=[jax.ShapeDtypeStruct(first.shape, F32)] * 3,
        input_output_aliases={7 + i: i for i in range(len(given))},
        compiler_params=pltpu.CompilerParams(vmem_limit_bytes=24 * 2**20),
        cost_estimate=pl.CostEstimate(flops=12 * units * width, bytes_accessed=34 * units * width, transcendentals=units * width),
    )(factors, keep, received, arrived, noise, first, second, *given)


def local(tokens, out_grad, gate_weight, up_weight, down_weight, counts, noise, first_moment, second_moment):
    model_width = tokens.shape[1]
    units = gate_weight.shape[1]
    hidden_units = units * lax.axis_size("mp")
    token_count = tokens.shape[0] * lax.axis_size("mp")
    member = lax.axis_index("client")
    core, far = member % 2, member // 2
    width = model_width // 4

    up_all = lax.all_gather(up_weight, "client", axis=0, tiled=True)
    down_all = lax.all_gather(down_weight, "client", axis=0, tiled=True)

    x_line, y_line = line_of(tokens, "dx"), line_of(out_grad, "dz")
    x_line, y_line = held(x_line, last_zeros(y_line)), held(y_line, last_zeros(x_line))
    *xs, x_low, x_high = ring(x_line, "dz")
    *ys, y_low, y_high = ring(y_line, "dx")
    gates, ups = [rows_dot(xs[0], gate_weight)], [rows_dot(xs[0], up_all)]
    x_far, y_far = far_block(x_low, x_high, "dz"), far_block(y_low, y_high, "dx")
    for x in xs[1:]:
        gates.append(rows_dot(x, gate_weight))
        ups.append(rows_dot(x, up_all))
    backs = [rows_dot(y, down_all) for y in ys]
    mark = token(*gates, *ups, *backs)
    x_far, y_far = held(x_far, mark), held(y_far, mark)
    xs.append(x_far)
    ys.append(y_far)
    gates.append(rows_dot(x_far, gate_weight))
    ups.append(rows_dot(x_far, up_all))
    backs.append(rows_dot(y_far, down_all))
    up_input, hidden = activations(gates, ups, backs, 2 * tokens.shape[0])

    here = jnp.stack([2 * far, 2 * (1 - far)])
    up_sent, down_sent, squares = deltas(xs, ys, up_input, hidden, here + (1 - core), width)
    up_received, down_received = swap_core(up_sent), swap_core(down_sent)
    up_kept, down_kept, more = deltas(xs, ys, up_input, hidden, here + core, width)

    client_total = jnp.full((8, 128), jnp.sum(squares + more), F32)
    client_total = client_total + flip(client_total, by=1)
    for axis in ("bx", "bz"):
        others = [flip(client_total, **{axis: b}) for b in (1, 2, 3)]
        client_total = (client_total + others[0]) + (others[1] + others[2])
    other_total = swap_core(client_total)
    clip_bound = math.sqrt(2.0 * model_width * hidden_units * token_count)
    weights = counts.astype(F32)
    shares = weights / jnp.sum(weights)
    norm_own, norm_other = jnp.sqrt(client_total[0, 0]), jnp.sqrt(other_total[0, 0])
    w_own = shares[member] * (clip_bound / jnp.maximum(norm_own, clip_bound))
    w_other = shares[member ^ 1] * (clip_bound / jnp.maximum(norm_other, clip_bound))
    most = w_own * norm_own + w_other * norm_other
    power = 14.0 - jnp.ceil(jnp.log2(jnp.where(most > 0.0, most, 1.0)))
    scale = jnp.exp2(jnp.clip(power, -100.0, 100.0))
    their_scale = swap_far(jnp.full((8, 128), scale, F32))[0, 0]
    factors = jnp.stack([w_own, w_other, 1.0 / their_scale])

    def weighted(kept, received, rows):
        total = (w_own * kept[1, rows] + w_other * received[1, rows]) * scale
        return total.astype(jnp.float16)

    cut = 256
    turn = lambda a: a.transpose(0, 2, 1)
    states = [turn(a) for a in (noise, first_moment, second_moment)]
    up_arrived = swap_far(weighted(up_kept, up_received, slice(None))).astype(F32)
    down_low = swap_far(weighted(down_kept, down_received, slice(0, cut))).astype(F32)
    outs = adam(0, 0, factors, up_kept, up_received, up_arrived, *states, None)
    down_high = weighted(down_kept, down_received, slice(cut, None))
    down_high = swap_far(held(down_high, jnp.minimum(jnp.abs(outs[0][0, :8, :128]), 0.0))).astype(F32)
    outs = adam(1, 0, factors, down_kept, down_received, down_low, *states, outs)
    outs = adam(1, cut, factors, down_kept, down_received, down_high, *states, outs)
    return tuple(turn(a) for a in outs)


def solution(mesh):
    state = P(None, "client", "mp")
    rows = P(("client", "mp"), None)
    placed = (rows, rows, P(None, "mp"), P("client", "mp"), P("client", "mp"), P(), state, state, state)
    return jax.shard_map(local, mesh=mesh, in_specs=placed, out_specs=(state,) * 3, check_vma=False)
```

```python
import math

import jax
import jax.numpy as jnp
from jax import lax
from jax.experimental import pallas as pl
from jax.experimental.pallas import tpu as pltpu
from jax.sharding import PartitionSpec as P

NX, NZ, NY = 4, 4, 2
BF16, F32 = jnp.bfloat16, jnp.float32
CORNER = (slice(0, 8), slice(0, 128))


def place(x, z, y):
    return (x % NX) * (NZ * NY) + (z % NZ) * NY + y % NY


def pairs(to):
    return [(place(x, z, y), place(*to(x, z, y))) for x in range(NX) for z in range(NZ) for y in range(NY)]


def send(value, dx=0, dz=0, dy=0):
    return lax.ppermute(value, "mp", pairs(lambda x, z, y: (x + dx, z + dz, y + dy)))


def flip(value, bx=0, bz=0, by=0):
    return lax.ppermute(value, "mp", pairs(lambda x, z, y: (x ^ bx, z ^ bz, y ^ by)))


def both(value, by):
    to = [((c, m), (c ^ 1, m ^ 1 if by else m)) for c in range(4) for m in range(NX * NZ * NY)]
    wide = NX * NZ * NY
    return lax.ppermute(value, ("client", "mp"), [(a[0] * wide + a[1], b[0] * wide + b[1]) for a, b in to])


def swap_core(value):
    return lax.ppermute(value, "client", [(c, c ^ 1) for c in range(4)])


def swap_far(value):
    return lax.ppermute(value, "client", [(c, c ^ 2) for c in range(4)])


def token(*others):
    corners = sum(jnp.abs(other[:8, :128].astype(F32)) for other in others)
    return swap_core(swap_core(jnp.minimum(corners, 0.0)))


def held(value, zeros):
    return value.at[:16, :128].add(jnp.concatenate([zeros, zeros]).astype(value.dtype))


def last_zeros(line):
    quarter = line.shape[0] // 4
    ends = [jnp.abs(line[at : at + 8, :128].astype(F32)) for at in (3 * quarter, 4 * quarter - 16)]
    return jnp.minimum(ends[0] + ends[1], 0.0)


def ring(block, axis):
    half = block.shape[0] // 2
    below = send(block, **{axis: 1})
    above = send(block, **{axis: -1})
    return [block, below, above, below[:half], above[half:]]


def far_block(low, high, axis):
    return jnp.concatenate([send(low, **{axis: 1}), send(high, **{axis: -1})], axis=0)


def line_of(own, axis):
    *blocks, low, high = ring(jnp.concatenate([own, send(own, dy=1)], axis=0), axis)
    return jnp.concatenate([*blocks, far_block(low, high, axis)], axis=0)


def rows_dot(rows, weight):
    return lax.dot_general(rows, weight, (((1,), (0,)), ((), ())), preferred_element_type=F32)


def activations(gates, ups, backs, cut):
    flat = [a for group in zip(gates, ups, backs) for a in group]
    units = flat[0].shape[1]
    rows = sum(a.shape[0] for a in gates)

    def kernel(*refs):
        ins, (up_input, hidden) = refs[: len(flat)], refs[len(flat) :]
        for i in range(4):
            for j in range(4):
                here, there = slice(j * cut, (j + 1) * cut), slice(i * cut, (i + 1) * cut)
                gate = ins[3 * i][here, :]
                silu = gate / (1.0 + jnp.exp(-gate))
                up_input[(4 * i + j) * cut : (4 * i + j + 1) * cut, :] = (ins[3 * j + 2][there, :] * silu).astype(BF16)
                hidden[(4 * j + i) * cut : (4 * j + i + 1) * cut, :] = (silu * ins[3 * i + 1][here, :]).astype(BF16)

    whole = pl.BlockSpec(memory_space=pltpu.VMEM)
    return pl.pallas_call(
        kernel,
        in_specs=[whole] * len(flat),
        out_specs=[whole] * 2,
        out_shape=[jax.ShapeDtypeStruct((rows, units), BF16)] * 2,
        compiler_params=pltpu.CompilerParams(vmem_limit_bytes=24 * 2**20),
        cost_estimate=pl.CostEstimate(flops=10 * rows * units, bytes_accessed=16 * rows * units, transcendentals=rows * units),
    )(*flat)


def deltas(xs, ys, up_input, hidden, columns, width, block=512):
    count, units, rows = len(xs), up_input.shape[1], up_input.shape[0]

    def kernel(_, *refs):
        x, y = refs[:count], refs[count : 2 * count]
        up_ref, hidden_ref, up_out, down_out, squares = refs[2 * count :]

        @pl.when((pl.program_id(0) == 0) & (pl.program_id(1) == 0))
        def _():
            squares[...] = jnp.zeros_like(squares)

        for left, pieces, out in ((up_ref, x, up_out), (hidden_ref, y, down_out)):
            right = jnp.concatenate([piece[...] for piece in pieces], axis=0)
            value = lax.dot_general(left[...], right, (((0,), (0,)), ((), ())), preferred_element_type=F32)
            out[0] = value
            folded = (value * value).reshape(units // 8, 8, block).sum(axis=0)
            squares[...] += sum(folded[:, 128 * i : 128 * (i + 1)] for i in range(block // 128))

    per = width // block
    read = lambda i, j, at: (0, at[i] * per + j)
    fixed = lambda i, j, at: (0, 0)
    return pl.pallas_call(
        kernel,
        grid_spec=pltpu.PrefetchScalarGridSpec(
            num_scalar_prefetch=1,
            grid=(2, per),
            in_specs=[pl.BlockSpec((p.shape[0], block), read) for p in (*xs, *ys)]
            + [pl.BlockSpec((rows, units), fixed)] * 2,
            out_specs=[pl.BlockSpec((1, units, block), lambda i, j, at: (i, 0, j))] * 2
            + [pl.BlockSpec((8, 128), fixed)],
        ),
        out_shape=[jax.ShapeDtypeStruct((2, units, width), F32)] * 2 + [jax.ShapeDtypeStruct((8, 128), F32)],
        compiler_params=pltpu.CompilerParams(vmem_limit_bytes=40 * 2**20),
        cost_estimate=pl.CostEstimate(
            flops=8 * rows * units * width, bytes_accessed=8 * rows * width + 16 * units * width, transcendentals=0
        ),
    )(columns, *xs, *ys, up_input, hidden)


def adam(index, row, factors, keep, received, arrived, noise, first, second, outs, block=64):
    units, width = arrived.shape
    base = row // block

    def kernel(factors, keep, received, arrived, noise, first, second, *refs):
        new_first, new_second, step = refs[-3:]
        average = noise[0].astype(F32) + (
            (factors[:1, :1] * keep[0] + factors[8:9, :1] * received[0]) + arrived[...] * factors[16:17, :1]
        )
        moment = 0.9 * first[0] + 0.1 * average
        spread = 0.99 * second[0] + 0.01 * average * average
        new_first[0] = moment
        new_second[0] = spread
        step[0] = moment / (jnp.sqrt(spread) + 0.001)

    zero = pl.BlockSpec((1, block, width), lambda i: (0, base + i, 0))
    mine = pl.BlockSpec((1, block, width), lambda i: (index, base + i, 0))
    given = () if outs is None else tuple(outs)
    return pl.pallas_call(
        kernel,
        grid=(units // block,),
        in_specs=[
            pl.BlockSpec((24, 128), lambda i: (0, 0)),
            zero,
            zero,
            pl.BlockSpec((block, width), lambda i: (i, 0)),
            mine,
            mine,
            mine,
        ]
        + [pl.BlockSpec(memory_space=pl.ANY)] * len(given),
        out_specs=[mine] * 3,
        out_shape=[jax.ShapeDtypeStruct(first.shape, F32)] * 3,
        input_output_aliases={7 + i: i for i in range(len(given))},
        compiler_params=pltpu.CompilerParams(vmem_limit_bytes=24 * 2**20),
        cost_estimate=pl.CostEstimate(flops=12 * units * width, bytes_accessed=34 * units * width, transcendentals=units * width),
    )(factors, keep, received, arrived, noise, first, second, *given)


def local(tokens, out_grad, gate_weight, up_weight, down_weight, counts, noise, first_moment, second_moment):
    model_width = tokens.shape[1]
    units = gate_weight.shape[1]
    hidden_units = units * lax.axis_size("mp")
    token_count = tokens.shape[0] * lax.axis_size("mp")
    member = lax.axis_index("client")
    core, far = member % 2, member // 2
    width = model_width // 4

    up_all = lax.all_gather(up_weight, "client", axis=0, tiled=True)
    down_all = lax.all_gather(down_weight, "client", axis=0, tiled=True)

    x_line, y_line = line_of(tokens, "dx"), line_of(out_grad, "dz")
    x_line, y_line = held(x_line, last_zeros(y_line)), held(y_line, last_zeros(x_line))
    *xs, x_low, x_high = ring(x_line, "dz")
    *ys, y_low, y_high = ring(y_line, "dx")
    gates, ups = [rows_dot(xs[0], gate_weight)], [rows_dot(xs[0], up_all)]
    x_far, y_far = far_block(x_low, x_high, "dz"), far_block(y_low, y_high, "dx")
    for x in xs[1:]:
        gates.append(rows_dot(x, gate_weight))
        ups.append(rows_dot(x, up_all))
    backs = [rows_dot(y, down_all) for y in ys]
    mark = token(*gates, *ups, *backs)
    x_far, y_far = held(x_far, mark), held(y_far, mark)
    xs.append(x_far)
    ys.append(y_far)
    gates.append(rows_dot(x_far, gate_weight))
    ups.append(rows_dot(x_far, up_all))
    backs.append(rows_dot(y_far, down_all))
    up_input, hidden = activations(gates, ups, backs, 2 * tokens.shape[0])

    here = jnp.stack([2 * far, 2 * (1 - far)])
    up_sent, down_sent, squares = deltas(xs, ys, up_input, hidden, here + (1 - core), width)
    up_received, down_received = swap_core(up_sent), swap_core(down_sent)
    up_kept, down_kept, more = deltas(xs, ys, up_input, hidden, here + core, width)

    partial = jnp.full((8, 128), jnp.sum(squares + more), F32)
    beside = flip(partial, by=1)
    across, aside = both(partial, False), both(partial, True)
    totals = jnp.concatenate([partial + beside, across + aside], axis=0)
    for axis in ("bx", "bz"):
        others = [flip(totals, **{axis: b}) for b in (1, 2, 3)]
        totals = (totals + others[0]) + (others[1] + others[2])
    clip_bound = math.sqrt(2.0 * model_width * hidden_units * token_count)
    weights = counts.astype(F32)
    shares = weights / jnp.sum(weights)
    share = jnp.repeat(jnp.stack([shares[member], shares[member ^ 1]]), 8)[:, None]
    norms = jnp.sqrt(totals)
    factor = share * (clip_bound / jnp.maximum(norms, clip_bound))
    most = factor[:8] * norms[:8] + factor[8:] * norms[8:]
    power = 14.0 - jnp.ceil(jnp.log2(jnp.where(most > 0.0, most, 1.0)))
    scale = jnp.exp2(jnp.clip(power, -100.0, 100.0))
    factors = jnp.concatenate([factor, 1.0 / swap_far(scale)], axis=0)
    w_own, w_other, scale = factor[:1, :1], factor[8:9, :1], scale[:1, :1]

    def weighted(kept, received, rows):
        total = (w_own * kept[1, rows] + w_other * received[1, rows]) * scale
        return total.astype(jnp.float16)

    cut = 256
    turn = lambda a: a.transpose(0, 2, 1)
    states = [turn(a) for a in (noise, first_moment, second_moment)]
    up_arrived = swap_far(weighted(up_kept, up_received, slice(None)))
    down = [weighted(down_kept, down_received, rows) for rows in (slice(0, cut), slice(cut, None))]
    down_low, down_high = lax.optimization_barrier(down)
    up_arrived = held(up_arrived, token(down_low, down_high)).astype(F32)
    down_low = swap_far(down_low).astype(F32)
    outs = adam(0, 0, factors, up_kept, up_received, up_arrived, *states, None)
    down_high = swap_far(held(down_high, jnp.minimum(jnp.abs(outs[0][0, :8, :128]), 0.0))).astype(F32)
    outs = adam(1, 0, factors, down_kept, down_received, down_low, *states, outs)
    outs = adam(1, cut, factors, down_kept, down_received, down_high, *states, outs)
    return tuple(turn(a) for a in outs)


def solution(mesh):
    state = P(None, "client", "mp")
    rows = P(("client", "mp"), None)
    placed = (rows, rows, P(None, "mp"), P("client", "mp"), P("client", "mp"), P(), state, state, state)
    return jax.shard_map(local, mesh=mesh, in_specs=placed, out_specs=(state,) * 3, check_vma=False)
```

```python
import math

import jax
import jax.numpy as jnp
from jax import lax
from jax.experimental import pallas as pl
from jax.experimental.pallas import tpu as pltpu
from jax.sharding import PartitionSpec as P

NX, NZ, NY = 4, 4, 2
BF16, F32 = jnp.bfloat16, jnp.float32
CORNER = (slice(0, 8), slice(0, 128))


def place(x, z, y):
    return (x % NX) * (NZ * NY) + (z % NZ) * NY + y % NY


def pairs(to):
    return [(place(x, z, y), place(*to(x, z, y))) for x in range(NX) for z in range(NZ) for y in range(NY)]


def send(value, dx=0, dz=0, dy=0):
    return lax.ppermute(value, "mp", pairs(lambda x, z, y: (x + dx, z + dz, y + dy)))


def flip(value, bx=0, bz=0, by=0):
    return lax.ppermute(value, "mp", pairs(lambda x, z, y: (x ^ bx, z ^ bz, y ^ by)))


def both(value, by):
    to = [((c, m), (c ^ 1, m ^ 1 if by else m)) for c in range(4) for m in range(NX * NZ * NY)]
    wide = NX * NZ * NY
    return lax.ppermute(value, ("client", "mp"), [(a[0] * wide + a[1], b[0] * wide + b[1]) for a, b in to])


def swap_core(value):
    return lax.ppermute(value, "client", [(c, c ^ 1) for c in range(4)])


def swap_far(value):
    return lax.ppermute(value, "client", [(c, c ^ 2) for c in range(4)])


def token(*others):
    corners = sum(jnp.abs(other[:8, :128].astype(F32)) for other in others)
    return swap_core(swap_core(jnp.minimum(corners, 0.0)))


def held(value, zeros):
    return value.at[:16, :128].add(jnp.concatenate([zeros, zeros]).astype(value.dtype))


def last_zeros(line):
    quarter = line.shape[0] // 4
    ends = [jnp.abs(line[at : at + 8, :128].astype(F32)) for at in (3 * quarter, 4 * quarter - 16)]
    return jnp.minimum(ends[0] + ends[1], 0.0)


def ring(block, axis):
    half = block.shape[0] // 2
    below = send(block, **{axis: 1})
    above = send(block, **{axis: -1})
    return [block, below, above, below[:half], above[half:]]


def far_block(low, high, axis):
    return jnp.concatenate([send(low, **{axis: 1}), send(high, **{axis: -1})], axis=0)


def line_of(own, axis):
    *blocks, low, high = ring(jnp.concatenate([own, send(own, dy=1)], axis=0), axis)
    return jnp.concatenate([*blocks, far_block(low, high, axis)], axis=0)


def rows_dot(rows, weight):
    return lax.dot_general(rows, weight, (((1,), (0,)), ((), ())), preferred_element_type=F32)


def activations(gates, ups, backs, cut):
    flat = [a for group in zip(gates, ups, backs) for a in group]
    units = flat[0].shape[1]
    rows = sum(a.shape[0] for a in gates)

    def kernel(*refs):
        ins, (up_input, hidden) = refs[: len(flat)], refs[len(flat) :]
        for i in range(4):
            for j in range(4):
                here, there = slice(j * cut, (j + 1) * cut), slice(i * cut, (i + 1) * cut)
                gate = ins[3 * i][here, :]
                silu = gate / (1.0 + jnp.exp(-gate))
                up_input[(4 * i + j) * cut : (4 * i + j + 1) * cut, :] = (ins[3 * j + 2][there, :] * silu).astype(BF16)
                hidden[(4 * j + i) * cut : (4 * j + i + 1) * cut, :] = (silu * ins[3 * i + 1][here, :]).astype(BF16)

    whole = pl.BlockSpec(memory_space=pltpu.VMEM)
    return pl.pallas_call(
        kernel,
        in_specs=[whole] * len(flat),
        out_specs=[whole] * 2,
        out_shape=[jax.ShapeDtypeStruct((rows, units), BF16)] * 2,
        compiler_params=pltpu.CompilerParams(vmem_limit_bytes=24 * 2**20),
        cost_estimate=pl.CostEstimate(flops=10 * rows * units, bytes_accessed=16 * rows * units, transcendentals=rows * units),
    )(*flat)


def deltas(xs, ys, up_input, hidden, columns, width, block=512):
    count, units, rows = len(xs), up_input.shape[1], up_input.shape[0]

    def kernel(_, *refs):
        x, y = refs[:count], refs[count : 2 * count]
        up_ref, hidden_ref, up_out, down_out, squares = refs[2 * count :]

        @pl.when((pl.program_id(0) == 0) & (pl.program_id(1) == 0))
        def _():
            squares[...] = jnp.zeros_like(squares)

        for left, pieces, out in ((up_ref, x, up_out), (hidden_ref, y, down_out)):
            right = jnp.concatenate([piece[...] for piece in pieces], axis=0)
            value = lax.dot_general(left[...], right, (((0,), (0,)), ((), ())), preferred_element_type=F32)
            out[0] = value
            folded = (value * value).reshape(units // 8, 8, block).sum(axis=0)
            squares[...] += sum(folded[:, 128 * i : 128 * (i + 1)] for i in range(block // 128))

    per = width // block
    read = lambda i, j, at: (0, at[i] * per + j)
    fixed = lambda i, j, at: (0, 0)
    return pl.pallas_call(
        kernel,
        grid_spec=pltpu.PrefetchScalarGridSpec(
            num_scalar_prefetch=1,
            grid=(2, per),
            in_specs=[pl.BlockSpec((p.shape[0], block), read) for p in (*xs, *ys)]
            + [pl.BlockSpec((rows, units), fixed)] * 2,
            out_specs=[pl.BlockSpec((1, units, block), lambda i, j, at: (i, 0, j))] * 2
            + [pl.BlockSpec((8, 128), fixed)],
        ),
        out_shape=[jax.ShapeDtypeStruct((2, units, width), F32)] * 2 + [jax.ShapeDtypeStruct((8, 128), F32)],
        compiler_params=pltpu.CompilerParams(vmem_limit_bytes=40 * 2**20),
        cost_estimate=pl.CostEstimate(
            flops=8 * rows * units * width, bytes_accessed=8 * rows * width + 16 * units * width, transcendentals=0
        ),
    )(columns, *xs, *ys, up_input, hidden)


def adam(index, row, factors, keep, received, arrived, noise, first, second, outs, block=64):
    units, width = arrived.shape
    base = row // block

    def kernel(factors, keep, received, arrived, noise, first, second, *refs):
        new_first, new_second, step = refs[-3:]
        average = noise[0].astype(F32) + (
            (factors[:1, :1] * keep[0] + factors[8:9, :1] * received[0]) + arrived[...] * factors[16:17, :1]
        )
        moment = 0.9 * first[0] + 0.1 * average
        spread = 0.99 * second[0] + 0.01 * average * average
        new_first[0] = moment
        new_second[0] = spread
        step[0] = moment / (jnp.sqrt(spread) + 0.001)

    zero = pl.BlockSpec((1, block, width), lambda i: (0, base + i, 0))
    mine = pl.BlockSpec((1, block, width), lambda i: (index, base + i, 0))
    given = () if outs is None else tuple(outs)
    return pl.pallas_call(
        kernel,
        grid=(units // block,),
        in_specs=[
            pl.BlockSpec((24, 128), lambda i: (0, 0)),
            zero,
            zero,
            pl.BlockSpec((block, width), lambda i: (i, 0)),
            mine,
            mine,
            mine,
        ]
        + [pl.BlockSpec(memory_space=pl.ANY)] * len(given),
        out_specs=[mine] * 3,
        out_shape=[jax.ShapeDtypeStruct(first.shape, F32)] * 3,
        input_output_aliases={7 + i: i for i in range(len(given))},
        compiler_params=pltpu.CompilerParams(vmem_limit_bytes=24 * 2**20),
        cost_estimate=pl.CostEstimate(flops=12 * units * width, bytes_accessed=34 * units * width, transcendentals=units * width),
    )(factors, keep, received, arrived, noise, first, second, *given)


def local(tokens, out_grad, gate_weight, up_weight, down_weight, counts, noise, first_moment, second_moment):
    model_width = tokens.shape[1]
    units = gate_weight.shape[1]
    hidden_units = units * lax.axis_size("mp")
    token_count = tokens.shape[0] * lax.axis_size("mp")
    member = lax.axis_index("client")
    core, far = member % 2, member // 2
    width = model_width // 4

    up_all = lax.all_gather(up_weight, "client", axis=0, tiled=True)
    down_all = lax.all_gather(down_weight, "client", axis=0, tiled=True)

    x_line, y_line = line_of(tokens, "dx"), line_of(out_grad, "dz")
    x_line, y_line = held(x_line, last_zeros(y_line)), held(y_line, last_zeros(x_line))
    *xs, x_low, x_high = ring(x_line, "dz")
    *ys, y_low, y_high = ring(y_line, "dx")
    gates, ups = [rows_dot(xs[0], gate_weight)], [rows_dot(xs[0], up_all)]
    x_far, y_far = far_block(x_low, x_high, "dz"), far_block(y_low, y_high, "dx")
    for x in xs[1:]:
        gates.append(rows_dot(x, gate_weight))
        ups.append(rows_dot(x, up_all))
    backs = [rows_dot(y, down_all) for y in ys]
    mark = token(*gates, *ups, *backs)
    x_far, y_far = held(x_far, mark), held(y_far, mark)
    xs.append(x_far)
    ys.append(y_far)
    gates.append(rows_dot(x_far, gate_weight))
    ups.append(rows_dot(x_far, up_all))
    backs.append(rows_dot(y_far, down_all))
    up_input, hidden = activations(gates, ups, backs, 2 * tokens.shape[0])

    here = jnp.stack([2 * far, 2 * (1 - far)])
    up_sent, down_sent, squares = deltas(xs, ys, up_input, hidden, here + (1 - core), width)
    up_received, down_received = swap_core(up_sent), swap_core(down_sent)
    up_kept, down_kept, more = deltas(xs, ys, up_input, hidden, here + core, width)

    partial = jnp.full((8, 128), jnp.sum(squares + more), F32)
    beside = flip(partial, by=1)
    across, aside = both(partial, False), both(partial, True)
    totals = jnp.concatenate([partial + beside, across + aside], axis=0)
    for axis in ("bx", "bz"):
        others = [flip(totals, **{axis: b}) for b in (1, 2, 3)]
        totals = (totals + others[0]) + (others[1] + others[2])
    clip_bound = math.sqrt(2.0 * model_width * hidden_units * token_count)
    weights = counts.astype(F32)
    shares = weights / jnp.sum(weights)
    share = jnp.repeat(jnp.stack([shares[member], shares[member ^ 1]]), 8)[:, None]
    norms = jnp.sqrt(totals)
    factor = share * (clip_bound / jnp.maximum(norms, clip_bound))
    most = factor[:8] * norms[:8] + factor[8:] * norms[8:]
    power = 14.0 - jnp.ceil(jnp.log2(jnp.where(most > 0.0, most, 1.0)))
    scale = jnp.exp2(jnp.clip(power, -100.0, 100.0))
    factors = jnp.concatenate([factor, 1.0 / swap_far(scale)], axis=0)
    w_own, w_other, scale = factor[:1, :1], factor[8:9, :1], scale[:1, :1]

    def weighted(kept, received, rows):
        total = (w_own * kept[1, rows] + w_other * received[1, rows]) * scale
        return total.astype(jnp.float16)

    cut = 320
    turn = lambda a: a.transpose(0, 2, 1)
    states = [turn(a) for a in (noise, first_moment, second_moment)]
    up_arrived = swap_far(weighted(up_kept, up_received, slice(None)))
    down = [weighted(down_kept, down_received, rows) for rows in (slice(0, cut), slice(cut, None))]
    down_low, down_high = lax.optimization_barrier(down)
    up_arrived = held(up_arrived, token(down_low, down_high)).astype(F32)
    down_low = swap_far(down_low).astype(F32)
    outs = adam(0, 0, factors, up_kept, up_received, up_arrived, *states, None)
    down_high = swap_far(held(down_high, jnp.minimum(jnp.abs(outs[0][0, :8, :128]), 0.0))).astype(F32)
    outs = adam(1, 0, factors, down_kept, down_received, down_low, *states, outs)
    outs = adam(1, cut, factors, down_kept, down_received, down_high, *states, outs)
    return tuple(turn(a) for a in outs)


def solution(mesh):
    state = P(None, "client", "mp")
    rows = P(("client", "mp"), None)
    placed = (rows, rows, P(None, "mp"), P("client", "mp"), P("client", "mp"), P(), state, state, state)
    return jax.shard_map(local, mesh=mesh, in_specs=placed, out_specs=(state,) * 3, check_vma=False)
```
